32 devices in a mesh: grp: 2 (over y), tm: 4 (over z), row: 4 (over x, core).
Axes of the slice: x: 2, y: 2, z: 4, core: 2. Of those that a mesh axis runs over, the one named last changes fastest.
Arguments:
- frames: bfloat16 [16, 8, 24, 512], P(('grp', 'tm'), 'row'), parts along dimension 0, may hold values from -6 to 6
- w_in: bfloat16 [3, 3, 512, 512], P(None, None, None, ('tm', 'row')), may hold values from -0.046875 to 0.046875
- w_out: bfloat16 [3, 3, 512, 512], P(None, None, None, ('tm', 'row')), may hold values from -0.09375 to 0.09375
- decay_codes: int32 [512], replicated, may hold values from 0 to 15
- resets: int32 [16], P(('grp', 'tm')), parts along dimension 0, may hold values from 0 to 1, as said below
Outputs:
- mixed: bfloat16 [16, 8, 24, 512], P(('grp', 'tm'), 'row'), parts along dimension 0
The draws below stay inside these ranges and needn't reach their ends.
There are 2 independent parts, one for each index of `grp`. The reference program is written for one: setup_inputs(seed, part) draws one part's arguments, and reference() takes and returns one part's arrays. A program takes and returns all parts, laid end to end along the dimension named above; an argument that names none is the same for every part. Nothing has to cross between parts.
Inputs may be any that keep to these rules, and one draw needn't show every extreme that they name: `decay_codes`: an entry of the table of 16 decays. `resets`: some frames start an episode and some do not.
All inputs are finite; a program needn't handle non-finite values.
Results may differ from the reference program's by a relative error of at most 0.005.
Values may be sent and summed in bfloat16 or wider, within the bound.
A program may use at most 64 MiB of HBM per device.

```python
import math
import jax
import jax.numpy as jnp
from jax import lax

C = 512
COLS = 24
LEVELS = 16
WINDOW = 4096
FRAMES = 8
HEIGHT = 8


def draw_resets(key, part):
    key_base, key_one, key_zero = jax.random.split(key, 3)
    rolled = jax.random.randint(key_base, (FRAMES,), 0, 6)
    base = (rolled == 0).astype(jnp.int32)
    first_pos = jax.random.randint(key_one, (), 0, FRAMES)
    offset = jax.random.randint(key_zero, (), 1, FRAMES)
    second_pos = (first_pos + offset) % FRAMES
    positions = jnp.arange(FRAMES, dtype=jnp.int32)
    with_one = jnp.where(positions == first_pos, 1, base)
    return jnp.where(positions == second_pos, 0, with_one).astype(jnp.int32)


def place_ends(array, rng, smallest, top_value):
    place = [jax.random.randint(jax.random.fold_in(rng, axis), (), 0, length) for axis, length in enumerate(array.shape)]
    longest = array.shape.index(max(array.shape))
    beside = place[:longest] + [(place[longest] + 1) % array.shape[longest]] + place[longest + 1:]
    return array.at[tuple(place)].set(smallest).at[tuple(beside)].set(top_value)


def block_scale(key, extent, cuts, low, top_value):
    gain, own = 1.0, jax.random.fold_in(key, 6)
    for position, shards_of in cuts:
        heights = jnp.exp(jax.random.uniform(jax.random.fold_in(own, position), (shards_of,), jnp.float32, low / len(cuts), top_value / len(cuts)))
        gain = gain * jnp.repeat(heights, extent[position] // shards_of).reshape([-1 if axis == position else 1 for axis in range(len(extent))])
    return gain


def noise(key, dims, deviation, reach, cuts=(), kind=jnp.bfloat16):
    factor_of = block_scale(key, dims, cuts, -0.22, 0.18) if cuts else 1.0
    values = jax.random.normal(key, dims, jnp.float32) * deviation * factor_of
    return jnp.minimum(jnp.maximum(values, -reach), reach).astype(kind)


def setup_inputs(seed: int = 0, part: int = 0) -> dict:
    arg_keys = jax.random.split(jax.random.key(seed), 6)
    part_splits = jax.random.split(jax.random.fold_in(arg_keys[5], part), 6)
    frames = noise(part_splits[0], (FRAMES, HEIGHT, COLS, C), 1.0, 6.0, ((0, 4), (1, 4)))
    w_in = noise(arg_keys[1], (3, 3, C, C), (36 * C) ** -0.5, 0.046875, ((3, 16),))
    w_out = noise(arg_keys[2], (3, 3, C, C), (9 * C) ** -0.5, 0.09375, ((3, 16),))
    decay_codes = place_ends(jax.random.randint(arg_keys[3], (C,), 0, LEVELS), jax.random.fold_in(arg_keys[3], 1), 0, LEVELS - 1).astype(jnp.int32)
    resets = draw_resets(jax.random.fold_in(jax.random.fold_in(arg_keys[5], part), 71), part)
    return dict(frames=frames, w_in=w_in, w_out=w_out, decay_codes=decay_codes, resets=resets)


LOW_LOG = math.log(0.995)
HIGH_LOG = math.log(0.9999)


def frame_rates(decay_codes, frame_count):
    levels = jnp.arange(LEVELS, dtype=jnp.int32)
    log_table = LOW_LOG + (levels.astype(jnp.float32) / (LEVELS - 1)) * (HIGH_LOG - LOW_LOG)
    picked = (decay_codes[:, None] == levels[None, :]).astype(jnp.float32)
    log_rate = jnp.sum(picked * log_table[None, :], axis=1)
    return jnp.exp((WINDOW / frame_count) * log_rate)


def conv_frame(image, weight):
    height, width = image.shape[0], image.shape[1]
    padded = jnp.pad(image, ((1, 1), (1, 1), (0, 0)))
    total = jnp.zeros((height * width, weight.shape[3]), jnp.float32)
    for i in range(3):
        for j in range(3):
            window = padded[i:i + height, j:j + width].reshape(height * width, -1)
            total = total + jnp.dot(window, weight[i, j], preferred_element_type=jnp.float32)
    return total.reshape(height, width, -1)


def reference(frames, w_in, w_out, decay_codes, resets):
    rates = frame_rates(decay_codes, FRAMES)
    gates = (1.0 - resets.astype(jnp.float32))[:, None] * rates[None, :]

    def advance(state, inputs):
        frame, gate = inputs
        drive = conv_frame(frame, w_in)
        state = gate[None, None, :] * state + drive
        hidden = jax.nn.gelu(state).astype(jnp.bfloat16)
        return state, conv_frame(hidden, w_out).astype(jnp.bfloat16)

    initial = jnp.zeros((HEIGHT, COLS, C), jnp.float32)
    _, mixed = lax.scan(advance, initial, (frames, gates))
    return mixed
```

```python
import math

import jax
import jax.numpy as jnp
from jax import lax
from jax.sharding import PartitionSpec as P

LEVELS = 16
WINDOW = 4096


LOW_LOG = math.log(0.995)
HIGH_LOG = math.log(0.9999)


def entering(part, axis, combine, identity):
    place = lax.axis_index(axis)
    gathered = jax.tree.map(lambda a: lax.all_gather(a, axis), part)
    state = jax.tree.map(lambda a, e: jnp.zeros_like(a) + jnp.asarray(e, a.dtype), part, identity)

    def one(turn, state):
        return combine(
            state, jax.tree.map(lambda a: lax.dynamic_index_in_dim(a, turn, 0, False), gathered)
        )

    return lax.fori_loop(0, place, one, state)


def extended_2(array, sides, width):
    for axis, dim in sides:
        size, length = (lax.axis_size(axis), array.shape[dim])
        up = [(i, (i + 1) % size) for i in range(size - 1)]
        down = [(j, i) for i, j in up]
        last = lax.slice_in_dim(array, length - width, length, axis=dim)
        initial = lax.slice_in_dim(array, 0, width, axis=dim)
        before = lax.ppermute(last, axis, up)
        after = lax.ppermute(initial, axis, down)
        array = jnp.concatenate([before, array, after], axis=dim)
    return array


def frame_rates(decay_codes, frame_count):
    levels = jnp.arange(LEVELS, dtype=jnp.int32)
    log_table = LOW_LOG + levels.astype(jnp.float32) / (LEVELS - 1) * (HIGH_LOG - LOW_LOG)
    picked = (decay_codes[:, None] == levels[None, :]).astype(jnp.float32)
    log_rate = jnp.sum(picked * log_table[None, :], axis=1)
    return jnp.exp(WINDOW / frame_count * log_rate)


def conv_rows(rows, weight):
    count, height, width = (rows.shape[0], rows.shape[1] - 2, rows.shape[2])
    padded = jnp.pad(rows, ((0, 0), (0, 0), (1, 1), (0, 0)))
    total = jnp.zeros((count, height, width, weight.shape[3]), jnp.float32)
    for i in range(3):
        for j in range(3):
            total = total + jnp.einsum(
                "frwc,ck->frwk",
                padded[:, i : i + height, j : j + width],
                weight[i, j],
                preferred_element_type=jnp.float32,
            )
    return total


def carry_combine(earlier, later):
    return (earlier[0] * later[0], later[0][None, None, :] * earlier[1] + later[1])


def recurrence(drive, gates):

    def advance(carry, inputs):
        state, product = carry
        frame_drive, gate = inputs
        state = gate[None, None, :] * state + frame_drive
        product = product * gate
        return ((state, product), (state, product))

    start = (jnp.zeros(drive.shape[1:], jnp.float32), jnp.ones((drive.shape[3],), jnp.float32))
    (last_state, last_product), (states, products) = lax.scan(advance, start, (drive, gates))
    identity = (jnp.ones_like(last_product), jnp.zeros_like(last_state))
    before_product, before_state = entering(
        (last_product, last_state), "tm", carry_combine, identity
    )
    return states + products[:, None, None, :] * before_state[None]


def by_filters(frames, w_in, w_out, decay_codes, resets):
    frame_count = frames.shape[0] * lax.axis_size("tm")
    rates = frame_rates(decay_codes, frame_count)
    gates = (1.0 - resets.astype(jnp.float32))[:, None] * rates[None, :]
    extended = extended_2(frames, (("row", 1),), 1)
    state = recurrence(
        conv_rows(extended, lax.all_gather(w_in, ("tm", "row"), axis=3, tiled=True)), gates
    )
    hidden = jax.nn.gelu(state).astype(jnp.bfloat16)
    hidden_rows = extended_2(hidden, (("row", 1),), 1)
    return conv_rows(hidden_rows, lax.all_gather(w_out, ("tm", "row"), axis=3, tiled=True)).astype(
        jnp.bfloat16
    )


def taps_matrix(weight):
    depth, width = weight.shape[2], weight.shape[3]
    return jnp.transpose(weight, (2, 0, 1, 3)).reshape(depth, 9 * width)


def conv_all(rows, weight):
    frames, height, width, depth = rows.shape
    out = weight.shape[3]
    taps = jnp.dot(
        rows.reshape(-1, depth), taps_matrix(weight), preferred_element_type=jnp.float32
    ).reshape(frames, height, width, 9 * out)
    padded = jnp.pad(taps, ((0, 0), (1, 1), (1, 1), (0, 0)))
    total = jnp.zeros((frames, height, width, out), jnp.float32)
    for i in range(3):
        for j in range(3):
            at = (3 * i + j) * out
            total = total + padded[:, i : i + height, j : j + width, at : at + out]
    return total


def by_activations(frames, w_in, w_out, decay_codes, resets):
    axes = ("tm", "row")
    tm, row = (lax.axis_size("tm"), lax.axis_size("row"))
    own, height, width, depth = frames.shape
    out = w_in.shape[3]
    count = own * tm
    place = lax.axis_index("tm") * row + lax.axis_index("row")
    codes = lax.dynamic_slice_in_dim(decay_codes, place * out, out)
    rates = frame_rates(codes, count)
    all_resets = lax.all_gather(resets.reshape(1, own), "tm", axis=0, tiled=True).reshape(count)
    gates = (1.0 - all_resets.astype(jnp.float32))[:, None] * rates[None, :]
    blocks = lax.all_gather(frames, axes, axis=0, tiled=False)
    blocks = blocks.reshape(tm, row, own, height, width, depth)
    everything = jnp.transpose(blocks, (0, 2, 1, 3, 4, 5)).reshape(
        count, row * height, width, depth
    )
    drive = conv_all(everything, w_in)
    state = jnp.zeros(drive.shape[1:], jnp.float32)
    hidden = []
    for t in range(count):
        state = gates[t][None, None, :] * state + drive[t]
        hidden.append(jax.nn.gelu(state).astype(jnp.bfloat16))
    hidden = lax.all_gather(jnp.stack(hidden), axes, axis=0, tiled=False)
    hidden = jnp.transpose(hidden, (1, 2, 3, 0, 4)).reshape(count, row * height, width, -1)
    mixed = conv_all(hidden, w_out).astype(jnp.bfloat16)
    parts = jnp.transpose(
        mixed.reshape(tm, own, row, height, width, out), (0, 2, 1, 3, 4, 5)
    ).reshape(tm * row, own, height, width, out)
    swapped = lax.all_to_all(parts, axes, 0, 0, tiled=True)
    return jnp.transpose(swapped, (1, 2, 3, 0, 4)).reshape(own, height, width, -1)


def on_device(frames, w_in, w_out, decay_codes, resets):
    devices = lax.axis_size("tm") * lax.axis_size("row")
    plan = by_activations if frames.size * devices < w_in.size * devices else by_filters
    return plan(frames, w_in, w_out, decay_codes, resets)


def solution(mesh):
    return jax.shard_map(
        on_device,
        mesh=mesh,
        in_specs=(
            P(("grp", "tm"), "row", None, None),
            P(None, None, None, ("tm", "row")),
            P(None, None, None, ("tm", "row")),
            P(),
            P(("grp", "tm")),
        ),
        out_specs=P(("grp", "tm"), "row", None, None),
        check_vma=False,
    )
```

```python
import functools
import math

import jax
import jax.numpy as jnp
from jax import lax
from jax.experimental import pallas as pl
from jax.experimental.pallas import tpu as pltpu
from jax.sharding import PartitionSpec as P

LEVELS = 16
WINDOW = 4096


LOW_LOG = math.log(0.995)
HIGH_LOG = math.log(0.9999)


def entering(part, axis, combine, identity):
    place = lax.axis_index(axis)
    gathered = jax.tree.map(lambda a: lax.all_gather(a, axis), part)
    state = jax.tree.map(lambda a, e: jnp.zeros_like(a) + jnp.asarray(e, a.dtype), part, identity)

    def one(turn, state):
        return combine(
            state, jax.tree.map(lambda a: lax.dynamic_index_in_dim(a, turn, 0, False), gathered)
        )

    return lax.fori_loop(0, place, one, state)


def extended_2(array, sides, width):
    for axis, dim in sides:
        size, length = (lax.axis_size(axis), array.shape[dim])
        up = [(i, (i + 1) % size) for i in range(size - 1)]
        down = [(j, i) for i, j in up]
        last = lax.slice_in_dim(array, length - width, length, axis=dim)
        initial = lax.slice_in_dim(array, 0, width, axis=dim)
        before = lax.ppermute(last, axis, up)
        after = lax.ppermute(initial, axis, down)
        array = jnp.concatenate([before, array, after], axis=dim)
    return array


def frame_rates(decay_codes, frame_count):
    levels = jnp.arange(LEVELS, dtype=jnp.int32)
    log_table = LOW_LOG + levels.astype(jnp.float32) / (LEVELS - 1) * (HIGH_LOG - LOW_LOG)
    picked = (decay_codes[:, None] == levels[None, :]).astype(jnp.float32)
    log_rate = jnp.sum(picked * log_table[None, :], axis=1)
    return jnp.exp(WINDOW / frame_count * log_rate)


def conv_rows(rows, weight):
    count, height, width = (rows.shape[0], rows.shape[1] - 2, rows.shape[2])
    padded = jnp.pad(rows, ((0, 0), (0, 0), (1, 1), (0, 0)))
    total = jnp.zeros((count, height, width, weight.shape[3]), jnp.float32)
    for i in range(3):
        for j in range(3):
            total = total + jnp.einsum(
                "frwc,ck->frwk",
                padded[:, i : i + height, j : j + width],
                weight[i, j],
                preferred_element_type=jnp.float32,
            )
    return total


def carry_combine(earlier, later):
    return (earlier[0] * later[0], later[0][None, None, :] * earlier[1] + later[1])


def recurrence(drive, gates):

    def advance(carry, inputs):
        state, product = carry
        frame_drive, gate = inputs
        state = gate[None, None, :] * state + frame_drive
        product = product * gate
        return ((state, product), (state, product))

    start = (jnp.zeros(drive.shape[1:], jnp.float32), jnp.ones((drive.shape[3],), jnp.float32))
    (last_state, last_product), (states, products) = lax.scan(advance, start, (drive, gates))
    identity = (jnp.ones_like(last_product), jnp.zeros_like(last_state))
    before_product, before_state = entering(
        (last_product, last_state), "tm", carry_combine, identity
    )
    return states + products[:, None, None, :] * before_state[None]


def by_filters(frames, w_in, w_out, decay_codes, resets):
    frame_count = frames.shape[0] * lax.axis_size("tm")
    rates = frame_rates(decay_codes, frame_count)
    gates = (1.0 - resets.astype(jnp.float32))[:, None] * rates[None, :]
    extended = extended_2(frames, (("row", 1),), 1)
    state = recurrence(
        conv_rows(extended, lax.all_gather(w_in, ("tm", "row"), axis=3, tiled=True)), gates
    )
    hidden = jax.nn.gelu(state).astype(jnp.bfloat16)
    hidden_rows = extended_2(hidden, (("row", 1),), 1)
    return conv_rows(hidden_rows, lax.all_gather(w_out, ("tm", "row"), axis=3, tiled=True)).astype(
        jnp.bfloat16
    )


MESH = pl.DeviceIdType.MESH
WIDE = 32
LANES = 128


def layer_kernel(
    tm,
    width,
    frames_ref,
    win_ref,
    wout_ref,
    codes_ref,
    resets_ref,
    out_ref,
    blocks,
    image,
    hidden_own,
    hidden_in,
    hidden,
    banks,
    keep,
    result_out,
    result_in,
    f_send,
    f_recv,
    k_send,
    k_recv,
    w_send,
    w_recv,
    e_send,
    e_recv,
    h_send,
    h_recv,
    o_send,
    o_recv,
    own_sem,
):
    z, r = (lax.axis_index("tm"), lax.axis_index("row"))
    rows = lax.axis_size("row")
    sibling = r + 1 - 2 * lax.rem(r, 2)
    partner = lax.rem(r + 2, 4)
    shard = win_ref.shape[2]
    own = frames_ref.shape[0] // (2 * width)
    count = own * tm
    depth = frames_ref.shape[1]
    started = []
    mine_copies = []

    def remote(src, dst, send, recv, **where):
        return pltpu.make_async_remote_copy(
            src_ref=src, dst_ref=dst, send_sem=send, recv_sem=recv,
            device_id=where, device_id_type=MESH,
        )

    barrier = pltpu.get_barrier_semaphore()
    for d in range(1, tm):
        pl.semaphore_signal(
            barrier, inc=1, device_id={"tm": lax.rem(z + d, tm)}, device_id_type=MESH
        )
    for d in range(1, rows):
        pl.semaphore_signal(
            barrier, inc=1, device_id={"row": lax.rem(r + d, rows)}, device_id_type=MESH
        )

    for f in range(own):
        keep[z, pl.ds(f, 1), :] = jnp.full(
            (1, LANES), 1.0 - resets_ref[f].astype(jnp.float32), jnp.float32
        )
    pl.semaphore_wait(barrier, tm + rows - 2)

    def bank_slot(b, i, place):
        return banks.at[b, i, :, pl.ds(pl.multiple_of(place * shard, shard), shard), :]

    def bank_sends(b, ref):
        copies = []
        for i in range(3):
            for kind, to in ((0, partner), (1, sibling)):
                copy = remote(
                    ref.at[i], bank_slot(b, i, r), w_send.at[b, kind, i], w_recv.at[b, kind, i],
                    row=to,
                )
                copy.start()
                copies.append(copy)
            mine = pltpu.make_async_copy(ref.at[i], bank_slot(b, i, r), own_sem.at[b, i])
            mine.start()
            mine_copies.append(mine)
        started.extend(c.wait_send for c in copies)
        return copies

    def bank_relay(b, i, copies):
        copies[2 * i].wait_recv()
        slot = bank_slot(b, i, partner)
        copy = remote(slot, slot, w_send.at[b, 2, i], w_recv.at[b, 2, i], row=sibling)
        copy.start()
        started.append(copy.wait_send)
        return copy

    def spread(make):
        copies = []
        for d in (1, tm - 1) + tuple(range(2, tm - 1)):
            copy = make(d, lax.rem(z + d, tm))
            copy.start()
            started.append(copy.wait_send)
            copies.append((d, copy))
        return copies

    def edge_copies(stage, array, d, part):
        slot = d + stage * tm
        up = remote(
            part(array, 1), part(array, 3), e_send.at[0, slot], e_recv.at[0, slot],
            row=jnp.maximum(r - 1, 0),
        )
        down = remote(
            part(array, 2), part(array, 0), e_send.at[1, slot], e_recv.at[1, slot],
            row=jnp.minimum(r + 1, rows - 1),
        )
        return (up, down)

    def start_edges(pair):
        @pl.when(r > 0)
        def _():
            pair[0].start()

        @pl.when(r < rows - 1)
        def _():
            pair[1].start()

    def wait_edges(pairs):
        @pl.when(r > 0)
        def _():
            for up, down in pairs:
                down.wait_recv()

        @pl.when(r < rows - 1)
        def _():
            for up, down in pairs:
                up.wait_recv()

    def finish_edges(pairs):
        @pl.when(r > 0)
        def _():
            for up, down in pairs:
                up.wait_send()

        @pl.when(r < rows - 1)
        def _():
            for up, down in pairs:
                down.wait_send()

    keeps = spread(
        lambda d, to: remote(keep.at[z], keep.at[z], k_send.at[d], k_recv.at[d], tm=to)
    )
    arriving = spread(
        lambda d, to: remote(frames_ref, blocks.at[z], f_send.at[d], f_recv.at[d], tm=to)
    )
    in_copies = bank_sends(0, win_ref)

    @pl.when(r == 0)
    def _():
        image[0] = jnp.zeros(image.shape[1:], image.dtype)
        hidden[0] = jnp.zeros(hidden.shape[1:], hidden.dtype)

    @pl.when(r == rows - 1)
    def _():
        image[3] = jnp.zeros(image.shape[1:], image.dtype)
        hidden[3] = jnp.zeros(hidden.shape[1:], hidden.dtype)

    gap = jnp.zeros((WIDE - width, depth), jnp.bfloat16)

    def place_frames(block, source):
        for f in range(own):
            for y in range(2):
                at = (2 * f + y) * width
                image[1 + y, source * own + f] = jnp.concatenate(
                    [block[at : at + width, :], gap], axis=0
                )

    def frame_part(source):
        return lambda array, y: array.at[y, pl.ds(source * own, own)]

    place_frames(frames_ref, z)
    edges = [edge_copies(0, image, 0, frame_part(z))]
    start_edges(edges[0])
    relays = []
    for n, (d, copy) in enumerate(arriving):
        copy.wait_recv()
        source = lax.rem(z - d + tm, tm)
        place_frames(blocks.at[source], source)
        pair = edge_copies(0, image, d, frame_part(source))
        start_edges(pair)
        edges.append(pair)
        if n < 3:
            relays.append(bank_relay(0, n, in_copies))
    for n in range(len(relays), 3):
        relays.append(bank_relay(0, n, in_copies))
    out_copies = bank_sends(1, wout_ref)
    for _, copy in keeps:
        copy.wait_recv()
    for n in range(3):
        in_copies[2 * n + 1].wait_recv()
        relays[n].wait_recv()
        mine_copies[n].wait()
    wait_edges(edges)

    def conv(array, b):
        total = None
        for i in range(3):
            term = lax.dot_general(
                array[i : i + 2].reshape(2 * count * WIDE, depth),
                banks[b, i].reshape(3 * LANES, depth),
                (((1,), (1,)), ((), ())),
                preferred_element_type=jnp.float32,
            )
            total = term if total is None else total + term
        size = 2 * count * WIDE
        left = pltpu.roll(total[:, :LANES], 1, 0)
        right = pltpu.roll(total[:, 2 * LANES :], size - 1, 0)
        return (left + total[:, LANES : 2 * LANES] + right).reshape(2, count, WIDE, LANES)

    drive = conv(image, 0)
    codes = codes_ref[:, pl.ds(pl.multiple_of(z * LANES, LANES), LANES)].astype(jnp.float32)
    rates = jnp.exp(
        WINDOW / count * (LOW_LOG + codes / (LEVELS - 1) * (HIGH_LOG - LOW_LOG))
    )
    state = jnp.zeros((2, width, LANES), jnp.float32)
    tail = jnp.zeros((2, WIDE - width, LANES), jnp.bfloat16)
    here = pl.ds(pl.multiple_of(z * LANES, LANES), LANES)
    for t in range(count):
        gate = keep[t // own, t % own : t % own + 1, :] * rates
        state = gate[None] * state + drive[:, t, :width]
        value = jax.nn.gelu(state).astype(jnp.bfloat16)
        hidden_own[t] = value.reshape(2 * width, LANES)
        hidden[1:3, t, :, here] = jnp.concatenate([value, tail], axis=1)

    arriving = spread(
        lambda d, to: remote(hidden_own, hidden_in.at[z], h_send.at[d], h_recv.at[d], tm=to)
    )

    def lane_part(source):
        lanes = pl.ds(pl.multiple_of(source * LANES, LANES), LANES)
        return lambda array, y: array.at[y, :, :, lanes]

    second = [edge_copies(1, hidden, 0, lane_part(z))]
    start_edges(second[0])
    relays = []
    for n, (d, copy) in enumerate(arriving):
        if n < 3:
            relays.append(bank_relay(1, n, out_copies))
        copy.wait_recv()
        source = lax.rem(z - d + tm, tm)
        lanes = pl.ds(pl.multiple_of(source * LANES, LANES), LANES)
        for t in range(count):
            value = hidden_in[source, t].reshape(2, width, LANES)
            hidden[1:3, t, :, lanes] = jnp.concatenate([value, tail], axis=1)
        pair = edge_copies(1, hidden, d, lane_part(source))
        start_edges(pair)
        second.append(pair)
    for n in range(len(relays), 3):
        relays.append(bank_relay(1, n, out_copies))
    for n in range(3):
        out_copies[2 * n + 1].wait_recv()
        relays[n].wait_recv()
    wait_edges(second)
    for n in range(3, 6):
        mine_copies[n].wait()
    mixed = conv(hidden, 1).astype(jnp.bfloat16)
    for k in range(tm):
        result_out[k] = jnp.concatenate(
            [mixed[y, k * own + f, :width] for f in range(own) for y in range(2)], axis=0
        )
    leaving = spread(
        lambda d, to: remote(
            result_out.at[to], result_in.at[z], o_send.at[d], o_recv.at[d], tm=to
        )
    )
    out_ref[:, here] = result_out[z]
    for d, copy in leaving:
        copy.wait_recv()
        source = lax.rem(z - d + tm, tm)
        out_ref[:, pl.ds(pl.multiple_of(source * LANES, LANES), LANES)] = result_in[source]
    for wait in started:
        wait()
    finish_edges(edges)
    finish_edges(second)


def by_channels(frames, w_in, w_out, decay_codes, resets):
    tm = lax.axis_size("tm")
    own, height, width, depth = frames.shape
    shard = w_in.shape[3]
    count = own * tm
    flat = own * height * width
    dma = pltpu.SemaphoreType.DMA
    vmem = pl.BlockSpec(memory_space=pltpu.VMEM)
    out = pl.pallas_call(
        functools.partial(layer_kernel, tm, width),
        out_shape=jax.ShapeDtypeStruct((flat, depth), jnp.bfloat16),
        in_specs=[vmem] * 4 + [pl.BlockSpec(memory_space=pltpu.SMEM)],
        out_specs=vmem,
        scratch_shapes=[
            pltpu.VMEM((tm, flat, depth), jnp.bfloat16),
            pltpu.VMEM((4, count, WIDE, depth), jnp.bfloat16),
            pltpu.VMEM((count, 2 * width, LANES), jnp.bfloat16),
            pltpu.VMEM((tm, count, 2 * width, LANES), jnp.bfloat16),
            pltpu.VMEM((4, count, WIDE, depth), jnp.bfloat16),
            pltpu.VMEM((2, 3, 3, 4 * shard, depth), jnp.bfloat16),
            pltpu.VMEM((tm, 8, LANES), jnp.float32),
            pltpu.VMEM((tm, flat, LANES), jnp.bfloat16),
            pltpu.VMEM((tm, flat, LANES), jnp.bfloat16),
            dma((tm,)),
            dma((tm,)),
            dma((tm,)),
            dma((tm,)),
            dma((2, 3, 3)),
            dma((2, 3, 3)),
            dma((2, 2 * tm)),
            dma((2, 2 * tm)),
            dma((tm,)),
            dma((tm,)),
            dma((tm,)),
            dma((tm,)),
            dma((2, 3)),
        ],
        compiler_params=pltpu.CompilerParams(
            collective_id=0, has_side_effects=True, vmem_limit_bytes=48 * 1024 * 1024
        ),
    )(
        frames.reshape(flat, depth),
        jnp.transpose(w_in, (0, 1, 3, 2)),
        jnp.transpose(w_out, (0, 1, 3, 2)),
        decay_codes.reshape(1, -1),
        resets,
    )
    return out.reshape(frames.shape)


def on_device(frames, w_in, w_out, decay_codes, resets):
    tm, row = (lax.axis_size("tm"), lax.axis_size("row"))
    own, height, width, depth = frames.shape
    fits = (
        row == 4
        and tm > 1
        and height == 2
        and own <= 8
        and width < WIDE
        and own * height * width % 16 == 0
        and 2 * width % 16 == 0
        and w_in.shape[3] * row == LANES
        and depth == tm * LANES
    )
    plan = by_channels if fits else by_filters
    return plan(frames, w_in, w_out, decay_codes, resets)


def solution(mesh):
    return jax.shard_map(
        on_device,
        mesh=mesh,
        in_specs=(
            P(("grp", "tm"), "row", None, None),
            P(None, None, None, ("tm", "row")),
            P(None, None, None, ("tm", "row")),
            P(),
            P(("grp", "tm")),
        ),
        out_specs=P(("grp", "tm"), "row", None, None),
        check_vma=False,
    )
```

```python
import functools
import math

import jax
import jax.numpy as jnp
from jax import lax
from jax.experimental import pallas as pl
from jax.experimental.pallas import tpu as pltpu
from jax.sharding import PartitionSpec as P

LEVELS = 16
WINDOW = 4096


LOW_LOG = math.log(0.995)
HIGH_LOG = math.log(0.9999)


def entering(part, axis, combine, identity):
    place = lax.axis_index(axis)
    gathered = jax.tree.map(lambda a: lax.all_gather(a, axis), part)
    state = jax.tree.map(lambda a, e: jnp.zeros_like(a) + jnp.asarray(e, a.dtype), part, identity)

    def one(turn, state):
        return combine(
            state, jax.tree.map(lambda a: lax.dynamic_index_in_dim(a, turn, 0, False), gathered)
        )

    return lax.fori_loop(0, place, one, state)


def extended_2(array, sides, width):
    for axis, dim in sides:
        size, length = (lax.axis_size(axis), array.shape[dim])
        up = [(i, (i + 1) % size) for i in range(size - 1)]
        down = [(j, i) for i, j in up]
        last = lax.slice_in_dim(array, length - width, length, axis=dim)
        initial = lax.slice_in_dim(array, 0, width, axis=dim)
        before = lax.ppermute(last, axis, up)
        after = lax.ppermute(initial, axis, down)
        array = jnp.concatenate([before, array, after], axis=dim)
    return array


def frame_rates(decay_codes, frame_count):
    levels = jnp.arange(LEVELS, dtype=jnp.int32)
    log_table = LOW_LOG + levels.astype(jnp.float32) / (LEVELS - 1) * (HIGH_LOG - LOW_LOG)
    picked = (decay_codes[:, None] == levels[None, :]).astype(jnp.float32)
    log_rate = jnp.sum(picked * log_table[None, :], axis=1)
    return jnp.exp(WINDOW / frame_count * log_rate)


def conv_rows(rows, weight):
    count, height, width = (rows.shape[0], rows.shape[1] - 2, rows.shape[2])
    padded = jnp.pad(rows, ((0, 0), (0, 0), (1, 1), (0, 0)))
    total = jnp.zeros((count, height, width, weight.shape[3]), jnp.float32)
    for i in range(3):
        for j in range(3):
            total = total + jnp.einsum(
                "frwc,ck->frwk",
                padded[:, i : i + height, j : j + width],
                weight[i, j],
                preferred_element_type=jnp.float32,
            )
    return total


def carry_combine(earlier, later):
    return (earlier[0] * later[0], later[0][None, None, :] * earlier[1] + later[1])


def recurrence(drive, gates):

    def advance(carry, inputs):
        state, product = carry
        frame_drive, gate = inputs
        state = gate[None, None, :] * state + frame_drive
        product = product * gate
        return ((state, product), (state, product))

    start = (jnp.zeros(drive.shape[1:], jnp.float32), jnp.ones((drive.shape[3],), jnp.float32))
    (last_state, last_product), (states, products) = lax.scan(advance, start, (drive, gates))
    identity = (jnp.ones_like(last_product), jnp.zeros_like(last_state))
    before_product, before_state = entering(
        (last_product, last_state), "tm", carry_combine, identity
    )
    return states + products[:, None, None, :] * before_state[None]


def by_filters(frames, w_in, w_out, decay_codes, resets):
    frame_count = frames.shape[0] * lax.axis_size("tm")
    rates = frame_rates(decay_codes, frame_count)
    gates = (1.0 - resets.astype(jnp.float32))[:, None] * rates[None, :]
    extended = extended_2(frames, (("row", 1),), 1)
    state = recurrence(
        conv_rows(extended, lax.all_gather(w_in, ("tm", "row"), axis=3, tiled=True)), gates
    )
    hidden = jax.nn.gelu(state).astype(jnp.bfloat16)
    hidden_rows = extended_2(hidden, (("row", 1),), 1)
    return conv_rows(hidden_rows, lax.all_gather(w_out, ("tm", "row"), axis=3, tiled=True)).astype(
        jnp.bfloat16
    )


MESH = pl.DeviceIdType.MESH
WIDE = 32
LANES = 128


def layer_kernel(
    tm,
    width,
    frames_ref,
    win_ref,
    wout_ref,
    codes_ref,
    resets_ref,
    out_ref,
    blocks,
    image,
    hidden_own,
    hidden_in,
    hidden,
    banks,
    keep,
    result_out,
    result_in,
    f_send,
    f_recv,
    k_send,
    k_recv,
    w_send,
    w_recv,
    e_send,
    e_recv,
    h_send,
    h_recv,
    o_send,
    o_recv,
    own_sem,
    codes_in,
):
    z, r = (lax.axis_index("tm"), lax.axis_index("row"))
    rows = lax.axis_size("row")
    sibling = r + 1 - 2 * lax.rem(r, 2)
    partner = lax.rem(r + 2, 4)
    shard = win_ref.shape[2]
    own = frames_ref.shape[0] // (2 * width)
    count = own * tm
    depth = frames_ref.shape[1]
    first = pltpu.make_async_copy(frames_ref, blocks.at[z], own_sem.at[0])
    first.start()
    table = pltpu.make_async_copy(codes_ref, codes_in, own_sem.at[1])
    table.start()
    started = []
    mine_copies = []

    def remote(src, dst, send, recv, **where):
        return pltpu.make_async_remote_copy(
            src_ref=src, dst_ref=dst, send_sem=send, recv_sem=recv,
            device_id=where, device_id_type=MESH,
        )

    barrier = pltpu.get_barrier_semaphore()
    for d in range(1, tm):
        pl.semaphore_signal(
            barrier, inc=1, device_id={"tm": lax.rem(z + d, tm)}, device_id_type=MESH
        )
    for d in range(1, rows):
        pl.semaphore_signal(
            barrier, inc=1, device_id={"row": lax.rem(r + d, rows)}, device_id_type=MESH
        )

    for f in range(own):
        keep[z, pl.ds(f, 1), :] = jnp.full(
            (1, LANES), 1.0 - resets_ref[f].astype(jnp.float32), jnp.float32
        )
    pl.semaphore_wait(barrier, tm + rows - 2)

    def bank_slot(b, i, place):
        return banks.at[b, i, :, pl.ds(pl.multiple_of(place * shard, shard), shard), :]

    def bank_sends(b, ref):
        copies = []
        for i in range(3):
            for kind, to in ((0, partner), (1, sibling)):
                copy = remote(
                    ref.at[i], bank_slot(b, i, r), w_send.at[b, kind, i], w_recv.at[b, kind, i],
                    row=to,
                )
                copy.start()
                copies.append(copy)
            mine = pltpu.make_async_copy(ref.at[i], bank_slot(b, i, r), own_sem.at[2 + 3 * b + i])
            mine.start()
            mine_copies.append(mine)
        started.extend(c.wait_send for c in copies)
        return copies

    def bank_relay(b, i, copies):
        copies[2 * i].wait_recv()
        slot = bank_slot(b, i, partner)
        copy = remote(slot, slot, w_send.at[b, 2, i], w_recv.at[b, 2, i], row=sibling)
        copy.start()
        started.append(copy.wait_send)
        return copy

    def spread(make):
        copies = []
        for d in (1, tm - 1) + tuple(range(2, tm - 1)):
            copy = make(d, lax.rem(z + d, tm))
            copy.start()
            started.append(copy.wait_send)
            copies.append((d, copy))
        return copies

    def line(origin, slots, send, recv, arrived, between):
        def hop(way, k):
            source = z - k if way == 0 else z + k
            to = z + 1 if way == 0 else z - 1
            src = origin if k == 0 else slots.at[source]
            return remote(
                src, slots.at[source], send.at[way, k], recv.at[way, k], tm=to
            )

        def sends(way, k):
            if way == 0:
                return (z >= k) & (z < tm - 1)
            return (z + k < tm) & (z > 0)

        def from_there(way, k):
            return z >= k if way == 0 else z + k < tm

        def when_start(way, k):
            @pl.when(sends(way, k))
            def _():
                hop(way, k).start()

        for way in range(2):
            when_start(way, 0)
        yield
        for k in range(1, tm):
            for way in range(2):
                source = z - k if way == 0 else z + k

                @pl.when(from_there(way, k))
                def _():
                    remote(
                        slots.at[source], slots.at[source], send.at[way, k], recv.at[way, k - 1],
                        tm=source,
                    ).wait_recv()
                    if k < tm - 1:
                        when_start(way, k)
                    arrived(source)

            between(k - 1)
        yield
        for way in range(2):
            for k in range(tm - 1):
                @pl.when(sends(way, k))
                def _():
                    hop(way, k).wait_send()
        yield

    def edge_copies(stage, array, source, part):
        slot = source + stage * tm
        up = remote(
            part(array, 1), part(array, 3), e_send.at[0, slot], e_recv.at[0, slot],
            row=jnp.maximum(r - 1, 0),
        )
        down = remote(
            part(array, 2), part(array, 0), e_send.at[1, slot], e_recv.at[1, slot],
            row=jnp.minimum(r + 1, rows - 1),
        )
        return (up, down)

    def start_edges(pair):
        @pl.when(r > 0)
        def _():
            pair[0].start()

        @pl.when(r < rows - 1)
        def _():
            pair[1].start()

    def wait_edges(pairs):
        @pl.when(r > 0)
        def _():
            for up, down in pairs:
                down.wait_recv()

        @pl.when(r < rows - 1)
        def _():
            for up, down in pairs:
                up.wait_recv()

    def finish_edges(pairs):
        @pl.when(r > 0)
        def _():
            for up, down in pairs:
                up.wait_send()

        @pl.when(r < rows - 1)
        def _():
            for up, down in pairs:
                down.wait_send()

    keeps = spread(
        lambda d, to: remote(keep.at[z], keep.at[z], k_send.at[d], k_recv.at[d], tm=to)
    )
    relays = []

    def frames_arrived(source):
        place_frames(blocks.at[source], source)
        start_edges(edge_copies(0, image, source, frame_part(source)))

    def relay_in(n):
        if n < 3:
            relays.append(bank_relay(0, n, in_copies))

    frames_line = line(frames_ref, blocks, f_send, f_recv, frames_arrived, relay_in)
    next(frames_line)
    in_copies = bank_sends(0, win_ref)

    @pl.when(r == 0)
    def _():
        image[0] = jnp.zeros(image.shape[1:], image.dtype)
        hidden[0] = jnp.zeros(hidden.shape[1:], hidden.dtype)

    @pl.when(r == rows - 1)
    def _():
        image[3] = jnp.zeros(image.shape[1:], image.dtype)
        hidden[3] = jnp.zeros(hidden.shape[1:], hidden.dtype)

    gap = jnp.zeros((WIDE - width, depth), jnp.bfloat16)

    def place_frames(block, source):
        for f in range(own):
            for y in range(2):
                at = (2 * f + y) * width
                image[1 + y, source * own + f] = jnp.concatenate(
                    [block[at : at + width, :], gap], axis=0
                )

    def frame_part(source):
        return lambda array, y: array.at[y, pl.ds(source * own, own)]

    first.wait()
    frames_arrived(z)
    next(frames_line)
    edges = [edge_copies(0, image, n, frame_part(n)) for n in range(tm)]
    for n in range(len(relays), 3):
        relays.append(bank_relay(0, n, in_copies))
    out_copies = bank_sends(1, wout_ref)
    for _, copy in keeps:
        copy.wait_recv()
    for n in range(3):
        in_copies[2 * n + 1].wait_recv()
        relays[n].wait_recv()
        mine_copies[n].wait()
    wait_edges(edges)

    def conv(array, b):
        total = None
        for i in range(3):
            term = lax.dot_general(
                array[i : i + 2].reshape(2 * count * WIDE, depth),
                banks[b, i].reshape(3 * LANES, depth),
                (((1,), (1,)), ((), ())),
                preferred_element_type=jnp.float32,
            )
            total = term if total is None else total + term
        size = 2 * count * WIDE
        left = pltpu.roll(total[:, :LANES], 1, 0)
        right = pltpu.roll(total[:, 2 * LANES :], size - 1, 0)
        return (left + total[:, LANES : 2 * LANES] + right).reshape(2, count, WIDE, LANES)

    drive = conv(image, 0)
    table.wait()
    codes = codes_in[:, pl.ds(pl.multiple_of(z * LANES, LANES), LANES)].astype(jnp.float32)
    rates = jnp.exp(
        WINDOW / count * (LOW_LOG + codes / (LEVELS - 1) * (HIGH_LOG - LOW_LOG))
    )
    state = jnp.zeros((2, width, LANES), jnp.float32)
    tail = jnp.zeros((2, WIDE - width, LANES), jnp.bfloat16)
    here = pl.ds(pl.multiple_of(z * LANES, LANES), LANES)
    for t in range(count):
        gate = keep[t // own, t % own : t % own + 1, :] * rates
        state = gate[None] * state + drive[:, t, :width]
        value = jax.nn.gelu(state).astype(jnp.bfloat16)
        hidden_own[t] = value.reshape(2 * width, LANES)
        hidden[1:3, t, :, here] = jnp.concatenate([value, tail], axis=1)

    def lane_part(source):
        at = source * LANES
        lanes = pl.ds(at if isinstance(at, int) else pl.multiple_of(at, LANES), LANES)
        return lambda array, y: array.at[y, :, :, lanes]

    relays = []

    def hidden_arrived(source):
        lanes = pl.ds(pl.multiple_of(source * LANES, LANES), LANES)
        for t in range(count):
            value = hidden_in[source, t].reshape(2, width, LANES)
            hidden[1:3, t, :, lanes] = jnp.concatenate([value, tail], axis=1)
        start_edges(edge_copies(1, hidden, source, lane_part(source)))

    def relay_out(n):
        if n < 3:
            relays.append(bank_relay(1, n, out_copies))

    hidden_line = line(hidden_own, hidden_in, h_send, h_recv, hidden_arrived, relay_out)
    next(hidden_line)
    start_edges(edge_copies(1, hidden, z, lane_part(z)))
    next(hidden_line)
    second = [
        edge_copies(1, hidden, n, lambda array, y, n=n: lane_part(n)(array, y)) for n in range(tm)
    ]
    for n in range(len(relays), 3):
        relays.append(bank_relay(1, n, out_copies))
    for n in range(3):
        out_copies[2 * n + 1].wait_recv()
        relays[n].wait_recv()
    wait_edges(second)
    for n in range(3, 6):
        mine_copies[n].wait()
    mixed = conv(hidden, 1).astype(jnp.bfloat16)
    for k in range(tm):
        result_out[k] = jnp.concatenate(
            [mixed[y, k * own + f, :width] for f in range(own) for y in range(2)], axis=0
        )
    leaving = spread(
        lambda d, to: remote(
            result_out.at[to], result_in.at[z], o_send.at[d], o_recv.at[d], tm=to
        )
    )
    out_ref[:, here] = result_out[z]
    for d, copy in leaving:
        copy.wait_recv()
        source = lax.rem(z - d + tm, tm)
        out_ref[:, pl.ds(pl.multiple_of(source * LANES, LANES), LANES)] = result_in[source]
    for wait in started:
        wait()
    next(frames_line)
    next(hidden_line)
    finish_edges(edges)
    finish_edges(second)


def by_channels(frames, w_in, w_out, decay_codes, resets):
    tm = lax.axis_size("tm")
    own, height, width, depth = frames.shape
    shard = w_in.shape[3]
    count = own * tm
    flat = own * height * width
    dma = pltpu.SemaphoreType.DMA
    vmem = pl.BlockSpec(memory_space=pltpu.VMEM)
    out = pl.pallas_call(
        functools.partial(layer_kernel, tm, width),
        out_shape=jax.ShapeDtypeStruct((flat, depth), jnp.bfloat16),
        in_specs=[pl.BlockSpec(memory_space=pl.ANY)] * 4 + [pl.BlockSpec(memory_space=pltpu.SMEM)],
        out_specs=vmem,
        scratch_shapes=[
            pltpu.VMEM((tm, flat, depth), jnp.bfloat16),
            pltpu.VMEM((4, count, WIDE, depth), jnp.bfloat16),
            pltpu.VMEM((count, 2 * width, LANES), jnp.bfloat16),
            pltpu.VMEM((tm, count, 2 * width, LANES), jnp.bfloat16),
            pltpu.VMEM((4, count, WIDE, depth), jnp.bfloat16),
            pltpu.VMEM((2, 3, 3, 4 * shard, depth), jnp.bfloat16),
            pltpu.VMEM((tm, 8, LANES), jnp.float32),
            pltpu.VMEM((tm, flat, LANES), jnp.bfloat16),
            pltpu.VMEM((tm, flat, LANES), jnp.bfloat16),
            dma((2, tm)),
            dma((2, tm)),
            dma((tm,)),
            dma((tm,)),
            dma((2, 3, 3)),
            dma((2, 3, 3)),
            dma((2, 2 * tm)),
            dma((2, 2 * tm)),
            dma((2, tm)),
            dma((2, tm)),
            dma((tm,)),
            dma((tm,)),
            dma((8,)),
            pltpu.VMEM((1, depth), jnp.int32),
        ],
        compiler_params=pltpu.CompilerParams(
            collective_id=0, has_side_effects=True, vmem_limit_bytes=60 * 1024 * 1024
        ),
    )(
        frames.reshape(flat, depth),
        jnp.transpose(w_in, (0, 1, 3, 2)),
        jnp.transpose(w_out, (0, 1, 3, 2)),
        decay_codes.reshape(1, -1),
        resets,
    )
    return out.reshape(frames.shape)


def on_device(frames, w_in, w_out, decay_codes, resets):
    tm, row = (lax.axis_size("tm"), lax.axis_size("row"))
    own, height, width, depth = frames.shape
    fits = (
        row == 4
        and tm > 1
        and height == 2
        and own <= 8
        and width < WIDE
        and own * height * width % 16 == 0
        and 2 * width % 16 == 0
        and w_in.shape[3] * row == LANES
        and depth == tm * LANES
    )
    plan = by_channels if fits else by_filters
    return plan(frames, w_in, w_out, decay_codes, resets)


def solution(mesh):
    return jax.shard_map(
        on_device,
        mesh=mesh,
        in_specs=(
            P(("grp", "tm"), "row", None, None),
            P(None, None, None, ("tm", "row")),
            P(None, None, None, ("tm", "row")),
            P(),
            P(("grp", "tm")),
        ),
        out_specs=P(("grp", "tm"), "row", None, None),
        check_vma=False,
    )
```

```python
import functools
import math

import jax
import jax.numpy as jnp
from jax import lax
from jax.experimental import pallas as pl
from jax.experimental.pallas import tpu as pltpu
from jax.sharding import PartitionSpec as P

LEVELS = 16
WINDOW = 4096


LOW_LOG = math.log(0.995)
HIGH_LOG = math.log(0.9999)


def entering(part, axis, combine, identity):
    place = lax.axis_index(axis)
    gathered = jax.tree.map(lambda a: lax.all_gather(a, axis), part)
    state = jax.tree.map(lambda a, e: jnp.zeros_like(a) + jnp.asarray(e, a.dtype), part, identity)

    def one(turn, state):
        return combine(
            state, jax.tree.map(lambda a: lax.dynamic_index_in_dim(a, turn, 0, False), gathered)
        )

    return lax.fori_loop(0, place, one, state)


def extended_2(array, sides, width):
    for axis, dim in sides:
        size, length = (lax.axis_size(axis), array.shape[dim])
        up = [(i, (i + 1) % size) for i in range(size - 1)]
        down = [(j, i) for i, j in up]
        last = lax.slice_in_dim(array, length - width, length, axis=dim)
        initial = lax.slice_in_dim(array, 0, width, axis=dim)
        before = lax.ppermute(last, axis, up)
        after = lax.ppermute(initial, axis, down)
        array = jnp.concatenate([before, array, after], axis=dim)
    return array


def frame_rates(decay_codes, frame_count):
    levels = jnp.arange(LEVELS, dtype=jnp.int32)
    log_table = LOW_LOG + levels.astype(jnp.float32) / (LEVELS - 1) * (HIGH_LOG - LOW_LOG)
    picked = (decay_codes[:, None] == levels[None, :]).astype(jnp.float32)
    log_rate = jnp.sum(picked * log_table[None, :], axis=1)
    return jnp.exp(WINDOW / frame_count * log_rate)


def conv_rows(rows, weight):
    count, height, width = (rows.shape[0], rows.shape[1] - 2, rows.shape[2])
    padded = jnp.pad(rows, ((0, 0), (0, 0), (1, 1), (0, 0)))
    total = jnp.zeros((count, height, width, weight.shape[3]), jnp.float32)
    for i in range(3):
        for j in range(3):
            total = total + jnp.einsum(
                "frwc,ck->frwk",
                padded[:, i : i + height, j : j + width],
                weight[i, j],
                preferred_element_type=jnp.float32,
            )
    return total


def carry_combine(earlier, later):
    return (earlier[0] * later[0], later[0][None, None, :] * earlier[1] + later[1])


def recurrence(drive, gates):

    def advance(carry, inputs):
        state, product = carry
        frame_drive, gate = inputs
        state = gate[None, None, :] * state + frame_drive
        product = product * gate
        return ((state, product), (state, product))

    start = (jnp.zeros(drive.shape[1:], jnp.float32), jnp.ones((drive.shape[3],), jnp.float32))
    (last_state, last_product), (states, products) = lax.scan(advance, start, (drive, gates))
    identity = (jnp.ones_like(last_product), jnp.zeros_like(last_state))
    before_product, before_state = entering(
        (last_product, last_state), "tm", carry_combine, identity
    )
    return states + products[:, None, None, :] * before_state[None]


def by_filters(frames, w_in, w_out, decay_codes, resets):
    frame_count = frames.shape[0] * lax.axis_size("tm")
    rates = frame_rates(decay_codes, frame_count)
    gates = (1.0 - resets.astype(jnp.float32))[:, None] * rates[None, :]
    extended = extended_2(frames, (("row", 1),), 1)
    state = recurrence(
        conv_rows(extended, lax.all_gather(w_in, ("tm", "row"), axis=3, tiled=True)), gates
    )
    hidden = jax.nn.gelu(state).astype(jnp.bfloat16)
    hidden_rows = extended_2(hidden, (("row", 1),), 1)
    return conv_rows(hidden_rows, lax.all_gather(w_out, ("tm", "row"), axis=3, tiled=True)).astype(
        jnp.bfloat16
    )


MESH = pl.DeviceIdType.MESH
WIDE = 32
LANES = 128


def layer_kernel(
    tm,
    width,
    frames_ref,
    win_ref,
    wout_ref,
    codes_ref,
    resets_ref,
    out_ref,
    blocks,
    image,
    hidden_own,
    hidden_in,
    hidden,
    banks,
    keep,
    result_out,
    result_in,
    f_send,
    f_recv,
    k_send,
    k_recv,
    w_send,
    w_recv,
    e_send,
    e_recv,
    h_send,
    h_recv,
    o_send,
    o_recv,
    own_sem,
    codes_in,
):
    z, r = (lax.axis_index("tm"), lax.axis_index("row"))
    rows = lax.axis_size("row")
    sibling = r + 1 - 2 * lax.rem(r, 2)
    partner = lax.rem(r + 2, 4)
    shard = win_ref.shape[2]
    own = frames_ref.shape[0] // (2 * width)
    count = own * tm
    depth = frames_ref.shape[1]
    first = pltpu.make_async_copy(frames_ref, blocks.at[z], own_sem.at[0])
    first.start()
    table = pltpu.make_async_copy(codes_ref, codes_in, own_sem.at[1])
    table.start()
    started = []
    mine_copies = []

    def remote(src, dst, send, recv, **where):
        return pltpu.make_async_remote_copy(
            src_ref=src, dst_ref=dst, send_sem=send, recv_sem=recv,
            device_id=where, device_id_type=MESH,
        )

    barrier = pltpu.get_barrier_semaphore()
    for d in range(1, tm):
        pl.semaphore_signal(
            barrier, inc=1, device_id={"tm": lax.rem(z + d, tm)}, device_id_type=MESH
        )
    for d in range(1, rows):
        pl.semaphore_signal(
            barrier, inc=1, device_id={"row": lax.rem(r + d, rows)}, device_id_type=MESH
        )

    for f in range(own):
        keep[z, pl.ds(f, 1), :] = jnp.full(
            (1, LANES), 1.0 - resets_ref[f].astype(jnp.float32), jnp.float32
        )
    pl.semaphore_wait(barrier, tm + rows - 2)

    def bank_slot(b, i, place):
        return banks.at[b, i, :, pl.ds(pl.multiple_of(place * shard, shard), shard), :]

    def bank_sends(b, ref):
        copies = []
        for i in range(3):
            for kind, to in ((0, partner), (1, sibling)):
                copy = remote(
                    ref.at[i], bank_slot(b, i, r), w_send.at[b, kind, i], w_recv.at[b, kind, i],
                    row=to,
                )
                copy.start()
                copies.append(copy)
            mine = pltpu.make_async_copy(ref.at[i], bank_slot(b, i, r), own_sem.at[2 + 3 * b + i])
            mine.start()
            mine_copies.append(mine)
        started.extend(c.wait_send for c in copies)
        return copies

    def bank_relay(b, i, copies):
        copies[2 * i].wait_recv()
        slot = bank_slot(b, i, partner)
        copy = remote(slot, slot, w_send.at[b, 2, i], w_recv.at[b, 2, i], row=sibling)
        copy.start()
        started.append(copy.wait_send)
        return copy

    def spread(make):
        copies = []
        for d in (1, tm - 1) + tuple(range(2, tm - 1)):
            copy = make(d, lax.rem(z + d, tm))
            copy.start()
            started.append(copy.wait_send)
            copies.append((d, copy))
        return copies

    def edge_copies(stage, array, d, part):
        slot = d + stage * tm
        up = remote(
            part(array, 1), part(array, 3), e_send.at[0, slot], e_recv.at[0, slot],
            row=jnp.maximum(r - 1, 0),
        )
        down = remote(
            part(array, 2), part(array, 0), e_send.at[1, slot], e_recv.at[1, slot],
            row=jnp.minimum(r + 1, rows - 1),
        )
        return (up, down)

    def start_edges(pair):
        @pl.when(r > 0)
        def _():
            pair[0].start()

        @pl.when(r < rows - 1)
        def _():
            pair[1].start()

    def wait_edges(pairs):
        @pl.when(r > 0)
        def _():
            for up, down in pairs:
                down.wait_recv()

        @pl.when(r < rows - 1)
        def _():
            for up, down in pairs:
                up.wait_recv()

    def finish_edges(pairs):
        @pl.when(r > 0)
        def _():
            for up, down in pairs:
                up.wait_send()

        @pl.when(r < rows - 1)
        def _():
            for up, down in pairs:
                down.wait_send()

    keeps = spread(
        lambda d, to: remote(keep.at[z], keep.at[z], k_send.at[d], k_recv.at[d], tm=to)
    )
    arriving = spread(
        lambda d, to: remote(frames_ref, blocks.at[z], f_send.at[d], f_recv.at[d], tm=to)
    )
    in_copies = bank_sends(0, win_ref)

    @pl.when(r == 0)
    def _():
        image[0] = jnp.zeros(image.shape[1:], image.dtype)
        hidden[0] = jnp.zeros(hidden.shape[1:], hidden.dtype)

    @pl.when(r == rows - 1)
    def _():
        image[3] = jnp.zeros(image.shape[1:], image.dtype)
        hidden[3] = jnp.zeros(hidden.shape[1:], hidden.dtype)

    gap = jnp.zeros((WIDE - width, depth), jnp.bfloat16)

    def place_frames(block, source):
        for f in range(own):
            for y in range(2):
                at = (2 * f + y) * width
                image[1 + y, source * own + f] = jnp.concatenate(
                    [block[at : at + width, :], gap], axis=0
                )

    def frame_part(source):
        return lambda array, y: array.at[y, pl.ds(source * own, own)]

    first.wait()
    place_frames(blocks.at[z], z)
    edges = [edge_copies(0, image, 0, frame_part(z))]
    start_edges(edges[0])
    relays = []
    for n, (d, copy) in enumerate(arriving):
        copy.wait_recv()
        source = lax.rem(z - d + tm, tm)
        place_frames(blocks.at[source], source)
        pair = edge_copies(0, image, d, frame_part(source))
        start_edges(pair)
        edges.append(pair)
        if n < 3:
            relays.append(bank_relay(0, n, in_copies))
    for n in range(len(relays), 3):
        relays.append(bank_relay(0, n, in_copies))
    out_copies = bank_sends(1, wout_ref)
    for _, copy in keeps:
        copy.wait_recv()
    for n in range(3):
        in_copies[2 * n + 1].wait_recv()
        relays[n].wait_recv()
        mine_copies[n].wait()

    def taps(rows, b, i):
        return lax.dot_general(
            rows.reshape(-1, depth),
            banks[b, i].reshape(3 * LANES, depth),
            (((1,), (1,)), ((), ())),
            preferred_element_type=jnp.float32,
        )

    def conv(array, b, pairs):
        inner = taps(array[1:3], b, 1)
        top = taps(array[2], b, 2)
        bottom = taps(array[1], b, 0)
        wait_edges(pairs)
        top = top + taps(array[0], b, 0)
        bottom = bottom + taps(array[3], b, 2)
        total = inner + jnp.concatenate([top, bottom], axis=0)
        size = 2 * count * WIDE
        left = pltpu.roll(total[:, :LANES], 1, 0)
        right = pltpu.roll(total[:, 2 * LANES :], size - 1, 0)
        return (left + total[:, LANES : 2 * LANES] + right).reshape(2, count, WIDE, LANES)

    drive = conv(image, 0, edges)
    table.wait()
    codes = codes_in[:, pl.ds(pl.multiple_of(z * LANES, LANES), LANES)].astype(jnp.float32)
    rates = jnp.exp(
        WINDOW / count * (LOW_LOG + codes / (LEVELS - 1) * (HIGH_LOG - LOW_LOG))
    )
    state = jnp.zeros((2, width, LANES), jnp.float32)
    tail = jnp.zeros((2, WIDE - width, LANES), jnp.bfloat16)
    here = pl.ds(pl.multiple_of(z * LANES, LANES), LANES)
    for t in range(count):
        gate = keep[t // own, t % own : t % own + 1, :] * rates
        state = gate[None] * state + drive[:, t, :width]
        value = jax.nn.gelu(state).astype(jnp.bfloat16)
        hidden_own[t] = value.reshape(2 * width, LANES)
        hidden[1:3, t, :, here] = jnp.concatenate([value, tail], axis=1)

    arriving = spread(
        lambda d, to: remote(hidden_own, hidden_in.at[z], h_send.at[d], h_recv.at[d], tm=to)
    )

    def lane_part(source):
        lanes = pl.ds(pl.multiple_of(source * LANES, LANES), LANES)
        return lambda array, y: array.at[y, :, :, lanes]

    second = [edge_copies(1, hidden, 0, lane_part(z))]
    start_edges(second[0])
    relays = []
    for n, (d, copy) in enumerate(arriving):
        if n < 3:
            relays.append(bank_relay(1, n, out_copies))
        copy.wait_recv()
        source = lax.rem(z - d + tm, tm)
        lanes = pl.ds(pl.multiple_of(source * LANES, LANES), LANES)
        for t in range(count):
            value = hidden_in[source, t].reshape(2, width, LANES)
            hidden[1:3, t, :, lanes] = jnp.concatenate([value, tail], axis=1)
        pair = edge_copies(1, hidden, d, lane_part(source))
        start_edges(pair)
        second.append(pair)
    for n in range(len(relays), 3):
        relays.append(bank_relay(1, n, out_copies))
    for n in range(3):
        out_copies[2 * n + 1].wait_recv()
        relays[n].wait_recv()
    for n in range(3, 6):
        mine_copies[n].wait()
    mixed = conv(hidden, 1, second).astype(jnp.bfloat16)
    for k in range(tm):
        result_out[k] = jnp.concatenate(
            [mixed[y, k * own + f, :width] for f in range(own) for y in range(2)], axis=0
        )
    leaving = spread(
        lambda d, to: remote(
            result_out.at[to], result_in.at[z], o_send.at[d], o_recv.at[d], tm=to
        )
    )
    out_ref[:, here] = result_out[z]
    for d, copy in leaving:
        copy.wait_recv()
        source = lax.rem(z - d + tm, tm)
        out_ref[:, pl.ds(pl.multiple_of(source * LANES, LANES), LANES)] = result_in[source]
    for wait in started:
        wait()
    finish_edges(edges)
    finish_edges(second)


def by_channels(frames, w_in, w_out, decay_codes, resets):
    tm = lax.axis_size("tm")
    own, height, width, depth = frames.shape
    shard = w_in.shape[3]
    count = own * tm
    flat = own * height * width
    dma = pltpu.SemaphoreType.DMA
    vmem = pl.BlockSpec(memory_space=pltpu.VMEM)
    out = pl.pallas_call(
        functools.partial(layer_kernel, tm, width),
        out_shape=jax.ShapeDtypeStruct((flat, depth), jnp.bfloat16),
        in_specs=[pl.BlockSpec(memory_space=pl.ANY)] * 4 + [pl.BlockSpec(memory_space=pltpu.SMEM)],
        out_specs=vmem,
        scratch_shapes=[
            pltpu.VMEM((tm, flat, depth), jnp.bfloat16),
            pltpu.VMEM((4, count, WIDE, depth), jnp.bfloat16),
            pltpu.VMEM((count, 2 * width, LANES), jnp.bfloat16),
            pltpu.VMEM((tm, count, 2 * width, LANES), jnp.bfloat16),
            pltpu.VMEM((4, count, WIDE, depth), jnp.bfloat16),
            pltpu.VMEM((2, 3, 3, 4 * shard, depth), jnp.bfloat16),
            pltpu.VMEM((tm, 8, LANES), jnp.float32),
            pltpu.VMEM((tm, flat, LANES), jnp.bfloat16),
            pltpu.VMEM((tm, flat, LANES), jnp.bfloat16),
            dma((tm,)),
            dma((tm,)),
            dma((tm,)),
            dma((tm,)),
            dma((2, 3, 3)),
            dma((2, 3, 3)),
            dma((2, 2 * tm)),
            dma((2, 2 * tm)),
            dma((tm,)),
            dma((tm,)),
            dma((tm,)),
            dma((tm,)),
            dma((8,)),
            pltpu.VMEM((1, depth), jnp.int32),
        ],
        compiler_params=pltpu.CompilerParams(
            collective_id=0, has_side_effects=True, vmem_limit_bytes=60 * 1024 * 1024
        ),
    )(
        frames.reshape(flat, depth),
        jnp.transpose(w_in, (0, 1, 3, 2)),
        jnp.transpose(w_out, (0, 1, 3, 2)),
        decay_codes.reshape(1, -1),
        resets,
    )
    return out.reshape(frames.shape)


def on_device(frames, w_in, w_out, decay_codes, resets):
    tm, row = (lax.axis_size("tm"), lax.axis_size("row"))
    own, height, width, depth = frames.shape
    fits = (
        row == 4
        and tm > 1
        and height == 2
        and own <= 8
        and width < WIDE
        and own * height * width % 16 == 0
        and 2 * width % 16 == 0
        and w_in.shape[3] * row == LANES
        and depth == tm * LANES
    )
    plan = by_channels if fits else by_filters
    return plan(frames, w_in, w_out, decay_codes, resets)


def solution(mesh):
    return jax.shard_map(
        on_device,
        mesh=mesh,
        in_specs=(
            P(("grp", "tm"), "row", None, None),
            P(None, None, None, ("tm", "row")),
            P(None, None, None, ("tm", "row")),
            P(),
            P(("grp", "tm")),
        ),
        out_specs=P(("grp", "tm"), "row", None, None),
        check_vma=False,
    )
```

```python
import functools
import math

import jax
import jax.numpy as jnp
from jax import lax
from jax.experimental import pallas as pl
from jax.experimental.pallas import tpu as pltpu
from jax.sharding import PartitionSpec as P

LEVELS = 16
WINDOW = 4096


LOW_LOG = math.log(0.995)
HIGH_LOG = math.log(0.9999)


def entering(part, axis, combine, identity):
    place = lax.axis_index(axis)
    gathered = jax.tree.map(lambda a: lax.all_gather(a, axis), part)
    state = jax.tree.map(lambda a, e: jnp.zeros_like(a) + jnp.asarray(e, a.dtype), part, identity)

    def one(turn, state):
        return combine(
            state, jax.tree.map(lambda a: lax.dynamic_index_in_dim(a, turn, 0, False), gathered)
        )

    return lax.fori_loop(0, place, one, state)


def extended_2(array, sides, width):
    for axis, dim in sides:
        size, length = (lax.axis_size(axis), array.shape[dim])
        up = [(i, (i + 1) % size) for i in range(size - 1)]
        down = [(j, i) for i, j in up]
        last = lax.slice_in_dim(array, length - width, length, axis=dim)
        initial = lax.slice_in_dim(array, 0, width, axis=dim)
        before = lax.ppermute(last, axis, up)
        after = lax.ppermute(initial, axis, down)
        array = jnp.concatenate([before, array, after], axis=dim)
    return array


def frame_rates(decay_codes, frame_count):
    levels = jnp.arange(LEVELS, dtype=jnp.int32)
    log_table = LOW_LOG + levels.astype(jnp.float32) / (LEVELS - 1) * (HIGH_LOG - LOW_LOG)
    picked = (decay_codes[:, None] == levels[None, :]).astype(jnp.float32)
    log_rate = jnp.sum(picked * log_table[None, :], axis=1)
    return jnp.exp(WINDOW / frame_count * log_rate)


def conv_rows(rows, weight):
    count, height, width = (rows.shape[0], rows.shape[1] - 2, rows.shape[2])
    padded = jnp.pad(rows, ((0, 0), (0, 0), (1, 1), (0, 0)))
    total = jnp.zeros((count, height, width, weight.shape[3]), jnp.float32)
    for i in range(3):
        for j in range(3):
            total = total + jnp.einsum(
                "frwc,ck->frwk",
                padded[:, i : i + height, j : j + width],
                weight[i, j],
                preferred_element_type=jnp.float32,
            )
    return total


def carry_combine(earlier, later):
    return (earlier[0] * later[0], later[0][None, None, :] * earlier[1] + later[1])


def recurrence(drive, gates):

    def advance(carry, inputs):
        state, product = carry
        frame_drive, gate = inputs
        state = gate[None, None, :] * state + frame_drive
        product = product * gate
        return ((state, product), (state, product))

    start = (jnp.zeros(drive.shape[1:], jnp.float32), jnp.ones((drive.shape[3],), jnp.float32))
    (last_state, last_product), (states, products) = lax.scan(advance, start, (drive, gates))
    identity = (jnp.ones_like(last_product), jnp.zeros_like(last_state))
    before_product, before_state = entering(
        (last_product, last_state), "tm", carry_combine, identity
    )
    return states + products[:, None, None, :] * before_state[None]


def by_filters(frames, w_in, w_out, decay_codes, resets):
    frame_count = frames.shape[0] * lax.axis_size("tm")
    rates = frame_rates(decay_codes, frame_count)
    gates = (1.0 - resets.astype(jnp.float32))[:, None] * rates[None, :]
    extended = extended_2(frames, (("row", 1),), 1)
    state = recurrence(
        conv_rows(extended, lax.all_gather(w_in, ("tm", "row"), axis=3, tiled=True)), gates
    )
    hidden = jax.nn.gelu(state).astype(jnp.bfloat16)
    hidden_rows = extended_2(hidden, (("row", 1),), 1)
    return conv_rows(hidden_rows, lax.all_gather(w_out, ("tm", "row"), axis=3, tiled=True)).astype(
        jnp.bfloat16
    )


MESH = pl.DeviceIdType.MESH
WIDE = 32
LANES = 128


def layer_kernel(
    tm,
    width,
    frames_ref,
    win_ref,
    wout_ref,
    codes_ref,
    resets_ref,
    out_ref,
    blocks,
    image,
    hidden_own,
    hidden_in,
    hidden,
    banks,
    keep,
    result_out,
    result_in,
    f_send,
    f_recv,
    k_send,
    k_recv,
    w_send,
    w_recv,
    e_send,
    e_recv,
    h_send,
    h_recv,
    o_send,
    o_recv,
    own_sem,
    codes_in,
):
    z, r = (lax.axis_index("tm"), lax.axis_index("row"))
    rows = lax.axis_size("row")
    sibling = r + 1 - 2 * lax.rem(r, 2)
    partner = lax.rem(r + 2, 4)
    shard = win_ref.shape[2]
    own = frames_ref.shape[0] // (2 * width)
    count = own * tm
    depth = frames_ref.shape[1]
    first = pltpu.make_async_copy(frames_ref, blocks.at[z], own_sem.at[0])
    first.start()
    table = pltpu.make_async_copy(codes_ref, codes_in, own_sem.at[1])
    table.start()
    started = []
    mine_copies = []

    def remote(src, dst, send, recv, **where):
        return pltpu.make_async_remote_copy(
            src_ref=src, dst_ref=dst, send_sem=send, recv_sem=recv,
            device_id=where, device_id_type=MESH,
        )

    barrier = pltpu.get_barrier_semaphore()
    for d in range(1, tm):
        pl.semaphore_signal(
            barrier, inc=1, device_id={"tm": lax.rem(z + d, tm)}, device_id_type=MESH
        )
    for d in range(1, rows):
        pl.semaphore_signal(
            barrier, inc=1, device_id={"row": lax.rem(r + d, rows)}, device_id_type=MESH
        )

    for f in range(own):
        keep[z, pl.ds(f, 1), :] = jnp.full(
            (1, LANES), 1.0 - resets_ref[f].astype(jnp.float32), jnp.float32
        )
    pl.semaphore_wait(barrier, tm + rows - 2)

    def bank_slot(b, i, place):
        return banks.at[b, i, :, pl.ds(pl.multiple_of(place * shard, shard), shard), :]

    def bank_sends(b, ref):
        copies = []
        for i in range(3):
            for kind, to in ((0, partner), (1, sibling)):
                copy = remote(
                    ref.at[i], bank_slot(b, i, r), w_send.at[b, kind, i], w_recv.at[b, kind, i],
                    row=to,
                )
                copy.start()
                copies.append(copy)
            mine = pltpu.make_async_copy(ref.at[i], bank_slot(b, i, r), own_sem.at[2 + 3 * b + i])
            mine.start()
            mine_copies.append(mine)
        started.extend(c.wait_send for c in copies)
        return copies

    def bank_relay(b, i, copies):
        copies[2 * i].wait_recv()
        slot = bank_slot(b, i, partner)
        copy = remote(slot, slot, w_send.at[b, 2, i], w_recv.at[b, 2, i], row=sibling)
        copy.start()
        started.append(copy.wait_send)
        return copy

    def spread(make):
        copies = []
        for d in (1, tm - 1) + tuple(range(2, tm - 1)):
            copy = make(d, lax.rem(z + d, tm))
            copy.start()
            started.append(copy.wait_send)
            copies.append((d, copy))
        return copies

    def edge_copies(stage, array, d, part):
        slot = d + stage * tm
        up = remote(
            part(array, 1), part(array, 3), e_send.at[0, slot], e_recv.at[0, slot],
            row=jnp.maximum(r - 1, 0),
        )
        down = remote(
            part(array, 2), part(array, 0), e_send.at[1, slot], e_recv.at[1, slot],
            row=jnp.minimum(r + 1, rows - 1),
        )
        return (up, down)

    def start_edges(pair):
        @pl.when(r > 0)
        def _():
            pair[0].start()

        @pl.when(r < rows - 1)
        def _():
            pair[1].start()

    def wait_edges(pairs):
        @pl.when(r > 0)
        def _():
            for up, down in pairs:
                down.wait_recv()

        @pl.when(r < rows - 1)
        def _():
            for up, down in pairs:
                up.wait_recv()

    def finish_edges(pairs):
        @pl.when(r > 0)
        def _():
            for up, down in pairs:
                up.wait_send()

        @pl.when(r < rows - 1)
        def _():
            for up, down in pairs:
                down.wait_send()

    keeps = spread(
        lambda d, to: remote(keep.at[z], keep.at[z], k_send.at[d], k_recv.at[d], tm=to)
    )
    arriving = spread(
        lambda d, to: remote(frames_ref, blocks.at[z], f_send.at[d], f_recv.at[d], tm=to)
    )
    in_copies = bank_sends(0, win_ref)

    @pl.when(r == 0)
    def _():
        image[0] = jnp.zeros(image.shape[1:], image.dtype)
        hidden[0] = jnp.zeros(hidden.shape[1:], hidden.dtype)

    @pl.when(r == rows - 1)
    def _():
        image[3] = jnp.zeros(image.shape[1:], image.dtype)
        hidden[3] = jnp.zeros(hidden.shape[1:], hidden.dtype)

    gap = jnp.zeros((WIDE - width, depth), jnp.bfloat16)

    def place_frames(block, source):
        for f in range(own):
            for y in range(2):
                at = (2 * f + y) * width
                image[1 + y, source * own + f] = jnp.concatenate(
                    [block[at : at + width, :], gap], axis=0
                )

    def frame_part(source):
        return lambda array, y: array.at[y, pl.ds(source * own, own)]

    first.wait()
    place_frames(blocks.at[z], z)
    edges = [edge_copies(0, image, 0, frame_part(z))]
    start_edges(edges[0])
    relays = []
    for n, (d, copy) in enumerate(arriving):
        copy.wait_recv()
        source = lax.rem(z - d + tm, tm)
        place_frames(blocks.at[source], source)
        pair = edge_copies(0, image, d, frame_part(source))
        start_edges(pair)
        edges.append(pair)
        if n < 3:
            relays.append(bank_relay(0, n, in_copies))
    for n in range(len(relays), 3):
        relays.append(bank_relay(0, n, in_copies))
    out_copies = bank_sends(1, wout_ref)
    for _, copy in keeps:
        copy.wait_recv()
    for n in range(3):
        in_copies[2 * n + 1].wait_recv()
        relays[n].wait_recv()
        mine_copies[n].wait()

    def taps(rows, b, i):
        return lax.dot_general(
            rows.reshape(-1, depth),
            banks[b, i].reshape(3 * LANES, depth),
            (((1,), (1,)), ((), ())),
            preferred_element_type=jnp.float32,
        )

    def conv(array, b, pairs):
        inner = taps(array[1:3], b, 1)
        top = taps(array[2], b, 2)
        bottom = taps(array[1], b, 0)
        wait_edges(pairs)
        top = top + taps(array[0], b, 0)
        bottom = bottom + taps(array[3], b, 2)
        total = inner + jnp.concatenate([top, bottom], axis=0)
        size = 2 * count * WIDE
        left = pltpu.roll(total[:, :LANES], 1, 0)
        right = pltpu.roll(total[:, 2 * LANES :], size - 1, 0)
        return (left + total[:, LANES : 2 * LANES] + right).reshape(2, count, WIDE, LANES)

    drive = conv(image, 0, edges)
    table.wait()
    codes = codes_in[:, pl.ds(pl.multiple_of(z * LANES, LANES), LANES)].astype(jnp.float32)
    rates = jnp.exp(
        WINDOW / count * (LOW_LOG + codes / (LEVELS - 1) * (HIGH_LOG - LOW_LOG))
    )
    state = jnp.zeros((2, width, LANES), jnp.float32)
    tail = jnp.zeros((2, WIDE - width, LANES), jnp.bfloat16)
    here = pl.ds(pl.multiple_of(z * LANES, LANES), LANES)
    piece = count // 2
    arriving, second = ([], [])

    def hidden_copy(part, d, to):
        frames_of = pl.ds(part * piece, piece)
        return remote(
            hidden_own.at[frames_of], hidden_in.at[z, frames_of],
            h_send.at[d + part * tm], h_recv.at[d + part * tm], tm=to,
        )

    def lane_part(source, part):
        lanes = pl.ds(pl.multiple_of(source * LANES, LANES), LANES)
        return lambda array, y: array.at[y, pl.ds(part * piece, piece), :, lanes]

    for t in range(count):
        gate = keep[t // own, t % own : t % own + 1, :] * rates
        state = gate[None] * state + drive[:, t, :width]
        value = jax.nn.gelu(state).astype(jnp.bfloat16)
        hidden_own[t] = value.reshape(2 * width, LANES)
        hidden[1:3, t, :, here] = jnp.concatenate([value, tail], axis=1)
        if (t + 1) % piece == 0:
            part = t // piece
            arriving.append(spread(functools.partial(hidden_copy, part)))
            pair = edge_copies(1 + part, hidden, 0, lane_part(z, part))
            start_edges(pair)
            second.append(pair)

    relays = []
    for part in range(2):
        for d, copy in arriving[part]:
            if len(relays) < 3:
                relays.append(bank_relay(1, len(relays), out_copies))
            copy.wait_recv()
            source = lax.rem(z - d + tm, tm)
            lanes = pl.ds(pl.multiple_of(source * LANES, LANES), LANES)
            for t in range(part * piece, (part + 1) * piece):
                value = hidden_in[source, t].reshape(2, width, LANES)
                hidden[1:3, t, :, lanes] = jnp.concatenate([value, tail], axis=1)
            pair = edge_copies(1 + part, hidden, d, lane_part(source, part))
            start_edges(pair)
            second.append(pair)
    for n in range(len(relays), 3):
        relays.append(bank_relay(1, n, out_copies))
    for n in range(3):
        out_copies[2 * n + 1].wait_recv()
        relays[n].wait_recv()
    for n in range(3, 6):
        mine_copies[n].wait()
    mixed = conv(hidden, 1, second).astype(jnp.bfloat16)
    for k in range(tm):
        result_out[k] = jnp.concatenate(
            [mixed[y, k * own + f, :width] for f in range(own) for y in range(2)], axis=0
        )
    leaving = spread(
        lambda d, to: remote(
            result_out.at[to], result_in.at[z], o_send.at[d], o_recv.at[d], tm=to
        )
    )
    out_ref[:, here] = result_out[z]
    for d, copy in leaving:
        copy.wait_recv()
        source = lax.rem(z - d + tm, tm)
        out_ref[:, pl.ds(pl.multiple_of(source * LANES, LANES), LANES)] = result_in[source]
    for wait in started:
        wait()
    finish_edges(edges)
    finish_edges(second)


def by_channels(frames, w_in, w_out, decay_codes, resets):
    tm = lax.axis_size("tm")
    own, height, width, depth = frames.shape
    shard = w_in.shape[3]
    count = own * tm
    flat = own * height * width
    dma = pltpu.SemaphoreType.DMA
    vmem = pl.BlockSpec(memory_space=pltpu.VMEM)
    out = pl.pallas_call(
        functools.partial(layer_kernel, tm, width),
        out_shape=jax.ShapeDtypeStruct((flat, depth), jnp.bfloat16),
        in_specs=[pl.BlockSpec(memory_space=pl.ANY)] * 4 + [pl.BlockSpec(memory_space=pltpu.SMEM)],
        out_specs=vmem,
        scratch_shapes=[
            pltpu.VMEM((tm, flat, depth), jnp.bfloat16),
            pltpu.VMEM((4, count, WIDE, depth), jnp.bfloat16),
            pltpu.VMEM((count, 2 * width, LANES), jnp.bfloat16),
            pltpu.VMEM((tm, count, 2 * width, LANES), jnp.bfloat16),
            pltpu.VMEM((4, count, WIDE, depth), jnp.bfloat16),
            pltpu.VMEM((2, 3, 3, 4 * shard, depth), jnp.bfloat16),
            pltpu.VMEM((tm, 8, LANES), jnp.float32),
            pltpu.VMEM((tm, flat, LANES), jnp.bfloat16),
            pltpu.VMEM((tm, flat, LANES), jnp.bfloat16),
            dma((tm,)),
            dma((tm,)),
            dma((tm,)),
            dma((tm,)),
            dma((2, 3, 3)),
            dma((2, 3, 3)),
            dma((2, 3 * tm)),
            dma((2, 3 * tm)),
            dma((2 * tm,)),
            dma((2 * tm,)),
            dma((tm,)),
            dma((tm,)),
            dma((8,)),
            pltpu.VMEM((1, depth), jnp.int32),
        ],
        compiler_params=pltpu.CompilerParams(
            collective_id=0, has_side_effects=True, vmem_limit_bytes=60 * 1024 * 1024
        ),
    )(
        frames.reshape(flat, depth),
        jnp.transpose(w_in, (0, 1, 3, 2)),
        jnp.transpose(w_out, (0, 1, 3, 2)),
        decay_codes.reshape(1, -1),
        resets,
    )
    return out.reshape(frames.shape)


def on_device(frames, w_in, w_out, decay_codes, resets):
    tm, row = (lax.axis_size("tm"), lax.axis_size("row"))
    own, height, width, depth = frames.shape
    fits = (
        row == 4
        and tm > 1
        and height == 2
        and own <= 8
        and own * tm % 2 == 0
        and width < WIDE
        and own * height * width % 16 == 0
        and 2 * width % 16 == 0
        and w_in.shape[3] * row == LANES
        and depth == tm * LANES
    )
    plan = by_channels if fits else by_filters
    return plan(frames, w_in, w_out, decay_codes, resets)


def solution(mesh):
    return jax.shard_map(
        on_device,
        mesh=mesh,
        in_specs=(
            P(("grp", "tm"), "row", None, None),
            P(None, None, None, ("tm", "row")),
            P(None, None, None, ("tm", "row")),
            P(),
            P(("grp", "tm")),
        ),
        out_specs=P(("grp", "tm"), "row", None, None),
        check_vma=False,
    )
```
